32 devices in a mesh: head: 4 (over y, core), ctx: 8 (over z, x).
Axes of the slice: x: 2, y: 2, z: 4, core: 2. Of those that a mesh axis runs over, the one named last changes fastest.
Arguments:
- query_states: bfloat16 [16384, 4096], P(('ctx', 'head')), may hold values from -8 to 8
- key_states: bfloat16 [16384, 1024], P(('ctx', 'head')), may hold values from -8 to 8
- value_states: bfloat16 [16384, 1024], P(('ctx', 'head')), may hold values from -6 to 6
- doc_lengths: int32 [16], replicated, may hold values from 1 to 6144, 16384 in all
- block_mask: int32 [32, 12], replicated, may hold values 0 or 1
Outputs:
- attended: bfloat16 [16384, 4096], P(('ctx', 'head'))
The draws below stay inside these ranges and needn't reach their ends.
Inputs may be any that keep to these rules, and one draw needn't show every extreme that they name: `doc_lengths`: the lengths sum to 16384; the longest document has exactly 6144 positions.
All inputs are finite; a program needn't handle non-finite values.
Results may differ from the reference program's by a relative error of at most 0.0035.
Values may be sent and summed in bfloat16 or wider, within the bound.
A program may use at most 128 MiB of HBM per device.

```python
import math
import jax
import jax.numpy as jnp
import numpy as np
from jax import lax

QHEADS = 32
KVHEADS = 8
HEAD_DIM = 128
BLOCK = 512
SEQ = 16384
NQB = 32
REACH_BLK = 13
MAXDOC = 6144
NDOCS = 16


def draw_query_states(key, part):
    result = jnp.clip(jax.random.normal(jax.random.fold_in(key, 3), (SEQ, QHEADS * HEAD_DIM), jnp.float32), -6.0, 6.0)
    return result.astype(jnp.bfloat16)


def draw_key_states(key, part):
    result = jnp.clip(jax.random.normal(jax.random.fold_in(key, 4), (SEQ, KVHEADS * HEAD_DIM), jnp.float32), -6.0, 6.0)
    return result.astype(jnp.bfloat16)


def place_ends(array, rng, low, high):
    longest = array.shape.index(max(array.shape))
    spots = []
    for shift in (0, 1):
        where = [jax.random.randint(jax.random.fold_in(rng, axis), (), 0, length) for axis, length in enumerate(array.shape)]
        where[longest] = (where[longest] + shift) % array.shape[longest]
        spots.append(tuple(where))
    return array.at[spots[0]].set(low).at[spots[1]].set(high)


def block_levels(rng, extent, cuts, low, largest):
    level, own = 1.0, jax.random.fold_in(rng, 6)
    for position, blocks in cuts:
        draws = jnp.exp(jax.random.uniform(jax.random.fold_in(own, position), (blocks,), jnp.float32, low / len(cuts), largest / len(cuts)))
        level = level * jnp.repeat(draws, extent[position] // blocks).reshape([-1 if axis == position else 1 for axis in range(len(extent))])
    return level


def profile(count, total, most, lean):
    portions = [(1 << 20) // math.isqrt(rank ** lean) + 1 for rank in range(2, count + 1)]
    spare, given = total - most - (count - 1), [1] * (count - 1)
    while spare > 0:
        candidates = [i for i in range(count - 1) if given[i] < most]
        pool, left = sum([portions[i] for i in candidates]), spare
        for i in candidates:
            addition = min(most - given[i], max(1, left * portions[i] // pool), spare)
            given[i] = given[i] + addition
            spare = spare - addition
    return np.array([most] + given)


def uneven_parts(key, number_of, total, bound, skew):
    if number_of == 2:
        one = jax.random.randint(key, (), max(1, total - bound), min(bound, total - 1) + 1)
        return jnp.stack([one, total - one])
    lengths = jnp.asarray(profile(number_of, total, bound, skew), jnp.int32)
    twos = (number_of - 1) // 2
    giver, taker = lengths[1:1 + 2 * twos:2], lengths[2:2 + 2 * twos:2]
    slack = jnp.minimum(giver - 1, bound - taker)
    passed = jax.random.randint(jax.random.fold_in(key, 1), (twos,), 0, 1 << 20) % (slack + 1)
    lengths = lengths.at[1:1 + 2 * twos:2].set(giver - passed).at[2:2 + 2 * twos:2].set(taker + passed)
    return lengths[jax.random.permutation(jax.random.fold_in(key, 2), number_of)]


def normal_values(stream_key, extent, width, bound, pieces=(), kind=jnp.bfloat16):
    array = jax.random.normal(stream_key, extent, jnp.float32) * width
    if len(pieces) > 0:
        array = block_levels(stream_key, extent, pieces, -0.22, 0.18) * array
    return jnp.clip(array, min=-bound, max=bound).astype(kind)


def setup_inputs(seed: int = 0) -> dict:
    arg_keys = jax.random.split(jax.random.key(seed), 6)
    query_states = draw_query_states(jax.random.fold_in(arg_keys[5], 71), 0)
    key_states = draw_key_states(jax.random.fold_in(arg_keys[5], 71), 0)
    value_states = normal_values(arg_keys[2], (SEQ, KVHEADS * HEAD_DIM), 1.0, 6.0, ((0, 32),))
    doc_lengths = uneven_parts(arg_keys[3], NDOCS, SEQ, MAXDOC, 2).astype(jnp.int32)
    block_mask = place_ends((jax.random.randint(arg_keys[4], (NQB, REACH_BLK - 1), 0, 2) < 1).astype(jnp.int32), jax.random.fold_in(arg_keys[4], 1), 0, 1)
    return {"query_states": query_states, "key_states": key_states, "value_states": value_states, "doc_lengths": doc_lengths, "block_mask": block_mask}


negative_fill = -1.0e30


def document_of(positions, starts):
    return jnp.sum((positions[:, None] >= starts[None, :]).astype(jnp.int32), axis=1) - 1


def reference(query_states, key_states, value_states, doc_lengths, block_mask):
    groups = QHEADS // KVHEADS
    score_scale = HEAD_DIM ** -0.5
    window_rows = REACH_BLK * BLOCK
    lead_rows = window_rows - BLOCK
    starts = jnp.cumsum(doc_lengths) - doc_lengths
    doc_ids = document_of(jnp.arange(SEQ, dtype=jnp.int32), starts)
    key_padded = jnp.concatenate([jnp.zeros((lead_rows, KVHEADS * HEAD_DIM), key_states.dtype), key_states], axis=0)
    value_padded = jnp.concatenate([jnp.zeros((lead_rows, KVHEADS * HEAD_DIM), value_states.dtype), value_states], axis=0)
    doc_padded = jnp.concatenate([jnp.full((lead_rows,), -1, jnp.int32), doc_ids])
    allowed_table = jnp.concatenate([jnp.ones((NQB, 1), jnp.int32), block_mask], axis=1)
    local_rows = jnp.arange(BLOCK, dtype=jnp.int32)
    window_local = jnp.arange(window_rows, dtype=jnp.int32)

    def block_output(block_index):
        row_start = block_index * BLOCK
        query_rows = lax.dynamic_slice_in_dim(query_states, row_start, BLOCK, 0).astype(jnp.float32)
        query_rows = jnp.moveaxis(query_rows.reshape(BLOCK, KVHEADS, groups, HEAD_DIM), 1, 0)
        key_rows = lax.dynamic_slice_in_dim(key_padded, row_start, window_rows, 0).astype(jnp.float32)
        key_rows = jnp.moveaxis(key_rows.reshape(window_rows, KVHEADS, HEAD_DIM), 1, 0)
        value_rows = lax.dynamic_slice_in_dim(value_padded, row_start, window_rows, 0).astype(jnp.float32)
        value_rows = jnp.moveaxis(value_rows.reshape(window_rows, KVHEADS, HEAD_DIM), 1, 0)
        key_docs = lax.dynamic_slice_in_dim(doc_padded, row_start, window_rows, 0)
        query_docs = lax.dynamic_slice_in_dim(doc_ids, row_start, BLOCK, 0)
        query_positions = row_start + local_rows
        key_positions = row_start - lead_rows + window_local
        allowed_row = lax.dynamic_index_in_dim(allowed_table, block_index, 0, keepdims=False)
        column_allowed = jnp.repeat(allowed_row[::-1], BLOCK)
        visible = (query_docs[:, None] == key_docs[None, :]) & (key_positions[None, :] <= query_positions[:, None]) & (column_allowed[None, :] == 1)
        visible = visible[:, None, :]

        def head_output(operands):
            head_queries, head_keys, head_values = operands
            scores = jnp.einsum("qgd,pd->qgp", head_queries, head_keys, precision=lax.Precision.HIGHEST) * score_scale
            row_top = jnp.max(jnp.where(visible, scores, negative_fill), axis=-1, keepdims=True)
            weights = jnp.where(visible, jnp.exp(scores - row_top), 0.0)
            weight_sum = jnp.sum(weights, axis=-1, keepdims=True)
            rounded = lax.optimization_barrier(weights.astype(jnp.bfloat16)).astype(jnp.float32)
            weighted = jnp.einsum("qgp,pd->qgd", rounded, head_values, precision=lax.Precision.HIGHEST)
            return (weighted / weight_sum).astype(jnp.bfloat16)

        per_head = lax.map(head_output, (query_rows, key_rows, value_rows))
        return jnp.moveaxis(per_head, 0, 1).reshape(BLOCK, QHEADS * HEAD_DIM)

    blocks = lax.map(block_output, jnp.arange(NQB, dtype=jnp.int32))
    return blocks.reshape(SEQ, QHEADS * HEAD_DIM)
```

```python
import functools

import jax
import jax.numpy as jnp
from jax import lax
from jax.experimental import pallas as pl
from jax.experimental.pallas import tpu as pltpu
from jax.sharding import PartitionSpec as P

HEAD_DIM = 128
BLOCK = 512
NEG = -1e30
LOG2E = 1.4426950408889634
AXES = ("ctx", "head")


def running_sum(values):
    at = jnp.arange(values.shape[-1], dtype=jnp.int32)
    return jnp.sum(jnp.where(at[:, None] > at[None, :], values[..., None, :], 0), axis=-1)


def start_of(positions, starts):
    return jnp.max(jnp.where(positions[..., None] >= starts, starts, 0), axis=-1)


def split_kernel(parts, qw, me_ref, q, k, v, *rest):
    outs, sems = rest[:-1], rest[-1]
    copies = []
    for i in range(parts):
        head = me_ref[0] ^ i
        kc = pl.ds(pl.multiple_of(head * HEAD_DIM, HEAD_DIM), HEAD_DIM)
        qc = pl.ds(pl.multiple_of(head * qw, qw), qw)
        copies.append(
            pltpu.make_async_copy(k.at[:, kc], outs[parts + i].at[:, pl.ds(0, HEAD_DIM)], sems.at[3 * i])
        )
        copies.append(
            pltpu.make_async_copy(
                v.at[:, kc], outs[parts + i].at[:, pl.ds(HEAD_DIM, HEAD_DIM)], sems.at[3 * i + 1]
            )
        )
        copies.append(pltpu.make_async_copy(q.at[:, qc], outs[i], sems.at[3 * i + 2]))
    for c in copies:
        c.start()
    for c in copies:
        c.wait()


def split_heads(place, query, key, value, parts):
    rows = query.shape[0]
    qw = query.shape[1] // parts
    hbm = pl.BlockSpec(memory_space=pl.ANY)
    return pl.pallas_call(
        functools.partial(split_kernel, parts, qw),
        out_shape=[jax.ShapeDtypeStruct((rows, qw), query.dtype)] * parts
        + [jax.ShapeDtypeStruct((rows, 2 * HEAD_DIM), key.dtype)] * parts,
        in_specs=[pl.BlockSpec(memory_space=pltpu.SMEM), hbm, hbm, hbm],
        out_specs=[hbm] * (2 * parts),
        scratch_shapes=[pltpu.SemaphoreType.DMA((3 * parts,))],
        name="split_heads",
    )(place, query, key, value)


def join_kernel(parts, qw, me_ref, *rest):
    pieces, out, sems = rest[:parts], rest[parts], rest[parts + 1]
    copies = []
    for i in range(parts):
        cols = pl.ds(pl.multiple_of((me_ref[0] ^ i) * qw, qw), qw)
        copies.append(pltpu.make_async_copy(pieces[i], out.at[:, cols], sems.at[i]))
    for c in copies:
        c.start()
    for c in copies:
        c.wait()


def join_heads(place, pieces):
    parts = len(pieces)
    rows, qw = pieces[0].shape
    hbm = pl.BlockSpec(memory_space=pl.ANY)
    return pl.pallas_call(
        functools.partial(join_kernel, parts, qw),
        out_shape=jax.ShapeDtypeStruct((rows, qw * parts), pieces[0].dtype),
        in_specs=[pl.BlockSpec(memory_space=pltpu.SMEM)] + [hbm] * parts,
        out_specs=hbm,
        scratch_shapes=[pltpu.SemaphoreType.DMA((parts,))],
        name="join_heads",
    )(place, *pieces)


def attend_kernel(groups, rows, cnt, ent, kbase, qbase, q_ref, st_ref, kv_ref, o_ref, m_ref, l_ref, acc_ref):
    t = pl.program_id(0)
    scale = HEAD_DIM ** (-0.5) * LOG2E
    m_ref[...] = jnp.full_like(m_ref, NEG)
    l_ref[...] = jnp.zeros_like(l_ref)
    acc_ref[...] = jnp.zeros_like(acc_ref)

    def tile(j, masked):
        row = pl.multiple_of((ent[t, j] >> 1) * rows, rows)
        k = kv_ref[pl.ds(row, rows), :HEAD_DIM]
        vt = kv_ref[pl.ds(row, rows), HEAD_DIM:].T
        if masked:
            kpos = kbase[t, j] + lax.broadcasted_iota(jnp.int32, (rows, rows), 0)
            qpos = qbase[t] + lax.broadcasted_iota(jnp.int32, (rows, rows), 1)
            visible = (kpos <= qpos) & (kpos >= st_ref[0])
        for g in range(groups):
            q = q_ref[0, :, g * HEAD_DIM : (g + 1) * HEAD_DIM]
            s = lax.dot_general(k, q, (((1,), (1,)), ((), ())), preferred_element_type=jnp.float32)
            if masked:
                s = jnp.where(visible, s, NEG)
            m_old = m_ref[g : g + 1]
            m_new = jnp.maximum(m_old, jnp.max(s, axis=0, keepdims=True))
            p = jnp.exp2((s - m_new) * scale)
            alpha = jnp.exp2((m_old - m_new) * scale)
            m_ref[g : g + 1] = m_new
            l_ref[g : g + 1] = l_ref[g : g + 1] * alpha + jnp.sum(p, axis=0, keepdims=True)
            o = lax.dot_general(
                vt, p.astype(jnp.bfloat16), (((1,), (0,)), ((), ())), preferred_element_type=jnp.float32
            )
            acc_ref[g] = acc_ref[g] * alpha + o

    def step(j, carry):
        @pl.when(ent[t, j] % 2 == 1)
        def _():
            tile(j, True)

        @pl.when(ent[t, j] % 2 == 0)
        def _():
            tile(j, False)

        return carry

    lax.fori_loop(0, cnt[t], step, 0)
    for g in range(groups):
        o = acc_ref[g] / l_ref[g : g + 1]
        o_ref[0, :, g * HEAD_DIM : (g + 1) * HEAD_DIM] = o.T.astype(o_ref.dtype)


def attend(tables, queries, row_starts, window):
    n, rows, qw = queries.shape
    groups = qw // HEAD_DIM
    return pl.pallas_call(
        functools.partial(attend_kernel, groups, rows),
        out_shape=jax.ShapeDtypeStruct(queries.shape, queries.dtype),
        grid_spec=pltpu.PrefetchScalarGridSpec(
            num_scalar_prefetch=4,
            grid=(n,),
            in_specs=[
                pl.BlockSpec((1, rows, qw), lambda t, *_: (t, 0, 0)),
                pl.BlockSpec((1, 1, rows), lambda t, *_: (t, 0, 0)),
                pl.BlockSpec(window.shape, lambda t, *_: (0, 0)),
            ],
            out_specs=pl.BlockSpec((1, rows, qw), lambda t, *_: (t, 0, 0)),
            scratch_shapes=[
                pltpu.VMEM((groups, rows), jnp.float32),
                pltpu.VMEM((groups, rows), jnp.float32),
                pltpu.VMEM((groups, HEAD_DIM, rows), jnp.float32),
            ],
        ),
        compiler_params=pltpu.CompilerParams(vmem_limit_bytes=40 * 2**20),
        cost_estimate=pl.CostEstimate(
            flops=n * 5 * 4 * rows * rows * qw, bytes_accessed=16 * 2**20, transcendentals=n * 5 * rows * rows * groups
        ),
        name="attend",
    )(*tables, queries, row_starts, window)


def tile_tables(group, place, parts, rows, lead_counts, doc_lengths, block_mask):
    starts = running_sum(doc_lengths)
    order = jnp.arange(parts, dtype=jnp.int32) ^ place
    q_tile = group * parts + order
    k_tile = [q_tile]
    for back, count in lead_counts:
        tiles = (group - back) * parts + order
        if count < parts:
            tiles = lax.dynamic_slice_in_dim(tiles, half_start(place, parts), count, 0)
        k_tile.append(tiles)
    k_tile = jnp.concatenate(k_tile)
    count = k_tile.shape[0]
    per = BLOCK // rows
    qb, kb = q_tile // per, k_tile // per
    offset = qb[:, None] - kb[None, :]
    allowed = jnp.concatenate([jnp.ones((block_mask.shape[0], 1), jnp.int32), block_mask], axis=1)[qb]
    reach = allowed.shape[1]
    hit = jnp.arange(reach, dtype=jnp.int32)
    allow = jnp.sum(
        jnp.where(offset[:, :, None] == hit, allowed[:, None, :], 0), axis=-1
    )
    q_rows = q_tile[:, None] * rows + jnp.arange(rows, dtype=jnp.int32)
    row_starts = start_of(q_rows, starts)
    k_first = k_tile * rows
    live = (
        (k_tile >= 0)[None, :]
        & (k_tile[None, :] <= q_tile[:, None])
        & (allow == 1)
        & ((k_first + rows - 1)[None, :] >= row_starts[:, :1])
    )
    masked = (k_tile[None, :] == q_tile[:, None]) | (k_first[None, :] < row_starts[:, -1:])
    live = live.astype(jnp.int32)
    spot = running_sum(live)
    pick = (spot[:, None, :] == jnp.arange(count, dtype=jnp.int32)[None, :, None]) & (live[:, None, :] == 1)
    code = jnp.arange(count, dtype=jnp.int32)[None, :] * 2 + masked.astype(jnp.int32)
    entries = jnp.sum(jnp.where(pick, code[:, None, :], 0), axis=-1)
    k_base = jnp.sum(jnp.where(pick, k_first[None, None, :], 0), axis=-1)
    return (jnp.sum(live, axis=1), entries, k_base, q_tile * rows), row_starts[:, None, :]


def half_start(place, parts):
    return jnp.where(place < parts // 2, parts // 2, 0)


def body(query_states, key_states, value_states, doc_lengths, block_mask):
    heads, ctxs = lax.axis_size("head"), lax.axis_size("ctx")
    devices = heads * ctxs
    parts = key_states.shape[1] // HEAD_DIM
    rows = query_states.shape[0]
    me = lax.axis_index("ctx") * heads + lax.axis_index("head")
    group, place = me // parts, me % parts
    span = (block_mask.shape[1] * BLOCK) // rows

    pieces = split_heads(place.reshape(1).astype(jnp.int32), query_states, key_states, value_states, parts)
    q_pieces, kv_pieces = pieces[:parts], pieces[parts:]

    def move(array, pairs):
        flat = [d % heads * ctxs + d // heads for d in range(devices)]
        return lax.ppermute(array, ("head", "ctx"), [(flat[a], flat[b]) for a, b in pairs])

    def swap(array, i):
        return move(array, [(d, d ^ i) for d in range(devices)]) if i else array

    kv_own = jnp.concatenate([swap(kv_pieces[i], i) for i in range(parts)], axis=0)
    window, lead_counts = [kv_own], []
    back = 1
    while span > 0:
        count = min(parts, span)
        sent = kv_own
        if count < parts:
            sent = lax.dynamic_slice_in_dim(kv_own, half_start(place, parts) * rows, count * rows, 0)
        shift = back * parts
        window.append(move(sent, [(d, d + shift) for d in range(devices - shift)]))
        lead_counts.append((back, count))
        span -= count
        back += 1
    window = jnp.concatenate(window, axis=0)
    q_own = jnp.stack([swap(q_pieces[i], i) for i in range(parts)])
    tables, row_starts = tile_tables(group, place, parts, rows, lead_counts, doc_lengths, block_mask)
    out = attend(tables, q_own, row_starts, window)
    back_pieces = [swap(out[i], i) for i in range(parts)]
    return join_heads(place.reshape(1).astype(jnp.int32), back_pieces)


def solution(mesh):
    placed = (P(AXES, None), P(AXES, None), P(AXES, None), P(), P())
    return jax.shard_map(body, mesh=mesh, in_specs=placed, out_specs=P(AXES, None), check_vma=False)
```

```python
import functools

import jax
import jax.numpy as jnp
from jax import lax
from jax.experimental import pallas as pl
from jax.experimental.pallas import tpu as pltpu
from jax.sharding import PartitionSpec as P

HEAD_DIM = 128
BLOCK = 512
NEG = -1e30
LOG2E = 1.4426950408889634
AXES = ("ctx", "head")


def running_sum(values):
    at = jnp.arange(values.shape[-1], dtype=jnp.int32)
    return jnp.sum(jnp.where(at[:, None] > at[None, :], values[..., None, :], 0), axis=-1)


def start_of(positions, starts):
    return jnp.max(jnp.where(positions[..., None] >= starts, starts, 0), axis=-1)


def split_kernel(parts, qw, me_ref, q, k, v, *rest):
    outs, sems = rest[:-1], rest[-1]
    copies = []
    for i in range(parts):
        head = me_ref[0] ^ i
        kc = pl.ds(pl.multiple_of(head * HEAD_DIM, HEAD_DIM), HEAD_DIM)
        qc = pl.ds(pl.multiple_of(head * qw, qw), qw)
        copies.append(
            pltpu.make_async_copy(k.at[:, kc], outs[parts + i].at[:, pl.ds(0, HEAD_DIM)], sems.at[3 * i])
        )
        copies.append(
            pltpu.make_async_copy(
                v.at[:, kc], outs[parts + i].at[:, pl.ds(HEAD_DIM, HEAD_DIM)], sems.at[3 * i + 1]
            )
        )
        copies.append(pltpu.make_async_copy(q.at[:, qc], outs[i], sems.at[3 * i + 2]))
    for c in copies:
        c.start()
    for c in copies:
        c.wait()


def split_heads(place, query, key, value, parts):
    rows = query.shape[0]
    qw = query.shape[1] // parts
    hbm = pl.BlockSpec(memory_space=pl.ANY)
    return pl.pallas_call(
        functools.partial(split_kernel, parts, qw),
        out_shape=[jax.ShapeDtypeStruct((rows, qw), query.dtype)] * parts
        + [jax.ShapeDtypeStruct((rows, 2 * HEAD_DIM), key.dtype)] * parts,
        in_specs=[pl.BlockSpec(memory_space=pltpu.SMEM)] + [pl.BlockSpec(memory_space=pltpu.VMEM)] * 3,
        out_specs=[hbm] * (2 * parts),
        scratch_shapes=[pltpu.SemaphoreType.DMA((3 * parts,))],
        name="split_heads",
    )(place, query, key, value)


def join_kernel(parts, qw, me_ref, *rest):
    pieces, out, sems = rest[:parts], rest[parts], rest[parts + 1]
    copies = []
    for i in range(parts):
        cols = pl.ds(pl.multiple_of((me_ref[0] ^ i) * qw, qw), qw)
        copies.append(pltpu.make_async_copy(pieces[i], out.at[:, cols], sems.at[i]))
    for c in copies:
        c.start()
    for c in copies:
        c.wait()


def join_heads(place, pieces):
    parts = len(pieces)
    rows, qw = pieces[0].shape
    hbm = pl.BlockSpec(memory_space=pl.ANY)
    return pl.pallas_call(
        functools.partial(join_kernel, parts, qw),
        out_shape=jax.ShapeDtypeStruct((rows, qw * parts), pieces[0].dtype),
        in_specs=[pl.BlockSpec(memory_space=pltpu.SMEM)] + [pl.BlockSpec(memory_space=pltpu.VMEM)] * parts,
        out_specs=hbm,
        scratch_shapes=[pltpu.SemaphoreType.DMA((parts,))],
        name="join_heads",
    )(place, *pieces)


def attend_kernel(groups, rows, cnt, ent, kbase, qbase, q_ref, st_ref, kv_ref, o_ref, m_ref, l_ref, acc_ref):
    t = pl.program_id(0)
    scale = HEAD_DIM ** (-0.5) * LOG2E
    m_ref[...] = jnp.full_like(m_ref, NEG)
    l_ref[...] = jnp.zeros_like(l_ref)
    acc_ref[...] = jnp.zeros_like(acc_ref)

    def tile(j, masked):
        row = pl.multiple_of((ent[t, j] >> 1) * rows, rows)
        k = kv_ref[pl.ds(row, rows), :HEAD_DIM]
        vt = kv_ref[pl.ds(row, rows), HEAD_DIM:].T
        if masked:
            kpos = kbase[t, j] + lax.broadcasted_iota(jnp.int32, (rows, rows), 0)
            qpos = qbase[t] + lax.broadcasted_iota(jnp.int32, (rows, rows), 1)
            visible = (kpos <= qpos) & (kpos >= st_ref[0])
        for g in range(groups):
            q = q_ref[0, :, g * HEAD_DIM : (g + 1) * HEAD_DIM]
            s = lax.dot_general(k, q, (((1,), (1,)), ((), ())), preferred_element_type=jnp.float32)
            if masked:
                s = jnp.where(visible, s, NEG)
            m_old = m_ref[g : g + 1]
            m_new = jnp.maximum(m_old, jnp.max(s, axis=0, keepdims=True))
            p = jnp.exp2((s - m_new) * scale)
            alpha = jnp.exp2((m_old - m_new) * scale)
            m_ref[g : g + 1] = m_new
            l_ref[g : g + 1] = l_ref[g : g + 1] * alpha + jnp.sum(p, axis=0, keepdims=True)
            o = lax.dot_general(
                vt, p.astype(jnp.bfloat16), (((1,), (0,)), ((), ())), preferred_element_type=jnp.float32
            )
            acc_ref[g] = acc_ref[g] * alpha + o

    def step(j, carry):
        @pl.when(ent[t, j] % 2 == 1)
        def _():
            tile(j, True)

        @pl.when(ent[t, j] % 2 == 0)
        def _():
            tile(j, False)

        return carry

    lax.fori_loop(0, cnt[t], step, 0)
    for g in range(groups):
        o = acc_ref[g] / l_ref[g : g + 1]
        o_ref[0, :, g * HEAD_DIM : (g + 1) * HEAD_DIM] = o.T.astype(o_ref.dtype)


def attend(tables, queries, row_starts, window):
    n, rows, qw = queries.shape
    groups = qw // HEAD_DIM
    return pl.pallas_call(
        functools.partial(attend_kernel, groups, rows),
        out_shape=jax.ShapeDtypeStruct(queries.shape, queries.dtype),
        grid_spec=pltpu.PrefetchScalarGridSpec(
            num_scalar_prefetch=4,
            grid=(n,),
            in_specs=[
                pl.BlockSpec((1, rows, qw), lambda t, *_: (t, 0, 0)),
                pl.BlockSpec((1, 1, rows), lambda t, *_: (t, 0, 0)),
                pl.BlockSpec(window.shape, lambda t, *_: (0, 0)),
            ],
            out_specs=pl.BlockSpec((1, rows, qw), lambda t, *_: (t, 0, 0)),
            scratch_shapes=[
                pltpu.VMEM((groups, rows), jnp.float32),
                pltpu.VMEM((groups, rows), jnp.float32),
                pltpu.VMEM((groups, HEAD_DIM, rows), jnp.float32),
            ],
        ),
        compiler_params=pltpu.CompilerParams(vmem_limit_bytes=40 * 2**20),
        cost_estimate=pl.CostEstimate(
            flops=n * 5 * 4 * rows * rows * qw, bytes_accessed=16 * 2**20, transcendentals=n * 5 * rows * rows * groups
        ),
        name="attend",
    )(*tables, queries, row_starts, window)


def tile_tables(group, place, parts, rows, lead_counts, doc_lengths, block_mask):
    starts = running_sum(doc_lengths)
    order = jnp.arange(parts, dtype=jnp.int32) ^ place
    q_tile = group * parts + order
    k_tile = [q_tile]
    for back, count in lead_counts:
        tiles = (group - back) * parts + order
        if count < parts:
            tiles = lax.dynamic_slice_in_dim(tiles, half_start(place, parts), count, 0)
        k_tile.append(tiles)
    k_tile = jnp.concatenate(k_tile)
    count = k_tile.shape[0]
    per = BLOCK // rows
    qb, kb = q_tile // per, k_tile // per
    offset = qb[:, None] - kb[None, :]
    allowed = jnp.concatenate([jnp.ones((block_mask.shape[0], 1), jnp.int32), block_mask], axis=1)[qb]
    reach = allowed.shape[1]
    hit = jnp.arange(reach, dtype=jnp.int32)
    allow = jnp.sum(
        jnp.where(offset[:, :, None] == hit, allowed[:, None, :], 0), axis=-1
    )
    q_rows = q_tile[:, None] * rows + jnp.arange(rows, dtype=jnp.int32)
    row_starts = start_of(q_rows, starts)
    k_first = k_tile * rows
    live = (
        (k_tile >= 0)[None, :]
        & (k_tile[None, :] <= q_tile[:, None])
        & (allow == 1)
        & ((k_first + rows - 1)[None, :] >= row_starts[:, :1])
    )
    masked = (k_tile[None, :] == q_tile[:, None]) | (k_first[None, :] < row_starts[:, -1:])
    live = live.astype(jnp.int32)
    spot = running_sum(live)
    pick = (spot[:, None, :] == jnp.arange(count, dtype=jnp.int32)[None, :, None]) & (live[:, None, :] == 1)
    code = jnp.arange(count, dtype=jnp.int32)[None, :] * 2 + masked.astype(jnp.int32)
    entries = jnp.sum(jnp.where(pick, code[:, None, :], 0), axis=-1)
    k_base = jnp.sum(jnp.where(pick, k_first[None, None, :], 0), axis=-1)
    return (jnp.sum(live, axis=1), entries, k_base, q_tile * rows), row_starts[:, None, :]


def half_start(place, parts):
    return jnp.where(place < parts // 2, parts // 2, 0)


def body(query_states, key_states, value_states, doc_lengths, block_mask):
    heads, ctxs = lax.axis_size("head"), lax.axis_size("ctx")
    devices = heads * ctxs
    parts = key_states.shape[1] // HEAD_DIM
    rows = query_states.shape[0]
    me = lax.axis_index("ctx") * heads + lax.axis_index("head")
    group, place = me // parts, me % parts
    span = (block_mask.shape[1] * BLOCK) // rows

    pieces = split_heads(place.reshape(1).astype(jnp.int32), query_states, key_states, value_states, parts)
    q_pieces, kv_pieces = pieces[:parts], pieces[parts:]

    def move(array, pairs):
        flat = [d % heads * ctxs + d // heads for d in range(devices)]
        return lax.ppermute(array, ("head", "ctx"), [(flat[a], flat[b]) for a, b in pairs])

    def swap(array, i):
        return move(array, [(d, d ^ i) for d in range(devices)]) if i else array

    kv_own = jnp.concatenate([swap(kv_pieces[i], i) for i in range(parts)], axis=0)
    window, lead_counts = [kv_own], []
    back = 1
    while span > 0:
        count = min(parts, span)
        sent = kv_own
        if count < parts:
            sent = lax.dynamic_slice_in_dim(kv_own, half_start(place, parts) * rows, count * rows, 0)
        shift = back * parts
        window.append(move(sent, [(d, d + shift) for d in range(devices - shift)]))
        lead_counts.append((back, count))
        span -= count
        back += 1
    window = jnp.concatenate(window, axis=0)
    q_own = jnp.stack([swap(q_pieces[i], i) for i in range(parts)])
    tables, row_starts = tile_tables(group, place, parts, rows, lead_counts, doc_lengths, block_mask)
    out = attend(tables, q_own, row_starts, window)
    back_pieces = [swap(out[i], i) for i in range(parts)]
    return join_heads(place.reshape(1).astype(jnp.int32), back_pieces)


def solution(mesh):
    placed = (P(AXES, None), P(AXES, None), P(AXES, None), P(), P())
    return jax.shard_map(body, mesh=mesh, in_specs=placed, out_specs=P(AXES, None), check_vma=False)
```

```python
import functools

import jax
import jax.numpy as jnp
from jax import lax
from jax.experimental import pallas as pl
from jax.experimental.pallas import tpu as pltpu
from jax.sharding import PartitionSpec as P

HEAD_DIM = 128
BLOCK = 512
NEG = -1e30
LOG2E = 1.4426950408889634
AXES = ("ctx", "head")


def running_sum(values):
    at = jnp.arange(values.shape[-1], dtype=jnp.int32)
    return jnp.sum(jnp.where(at[:, None] > at[None, :], values[..., None, :], 0), axis=-1)


def start_of(positions, starts):
    return jnp.max(jnp.where(positions[..., None] >= starts, starts, 0), axis=-1)


def gather_kernel(heads, parts, groups, leads, q, k, v, q_all, k_win, v_win, own_sem, qs, qr, ks, kr, zs, zr):
    rows = q.shape[0]
    qw = q.shape[1] // parts
    me = lax.axis_index("ctx") * heads + lax.axis_index("head")
    group, place = me // parts, me % parts
    has_next = group + 1 < groups

    def device(where):
        return {"ctx": where // heads, "head": where % heads}

    def partner(i):
        return group * parts + (place + i) % parts

    barrier = pltpu.get_barrier_semaphore()
    for i in range(1, parts):
        pl.semaphore_signal(barrier, inc=1, device_id=device(partner(i)), device_id_type=pl.DeviceIdType.MESH)

    for step in (1, groups - 1):
        pl.semaphore_signal(
            barrier,
            inc=1,
            device_id=device((group + step) % groups * parts + place),
            device_id_type=pl.DeviceIdType.MESH,
        )
    pl.semaphore_wait(barrier, parts + 1)

    def lanes(at, width):
        return pl.ds(pl.multiple_of(at * width, width), width)

    def window_rows(at):
        return pl.ds(pl.multiple_of(at * rows, rows), rows)

    wins = ((k, k_win), (v, v_win))

    def remote(src, dst, send, recv, where):
        return pltpu.make_async_remote_copy(
            src_ref=src,
            dst_ref=dst,
            send_sem=send,
            recv_sem=recv,
            device_id=device(where),
            device_id_type=pl.DeviceIdType.MESH,
        )

    def kv_swap(i, n):
        to = (place + i) % parts
        src, win = wins[n]
        return remote(
            src.at[:, lanes(to, HEAD_DIM)], win.at[window_rows(place)], ks.at[n, i], kr.at[n, i], partner(i)
        )

    def kv_arrival(i, n):
        win = wins[n][1].at[window_rows((place + parts - i) % parts)]
        return remote(win, win, ks.at[n, i], kr.at[n, i], partner(i))

    def q_swap(i):
        to = (place + i) % parts
        return remote(q.at[:, lanes(to, qw)], q_all.at[place], qs.at[i], qr.at[i], partner(i))

    def q_arrival(i):
        tile = q_all.at[(place + parts - i) % parts]
        return remote(tile, tile, qs.at[i], qr.at[i], partner(i))

    own = [
        pltpu.make_async_copy(src.at[:, lanes(place, HEAD_DIM)], win.at[window_rows(place)], own_sem.at[n])
        for n, (src, win) in enumerate(wins)
    ]
    own.append(pltpu.make_async_copy(q.at[:, lanes(place, qw)], q_all.at[place], own_sem.at[2]))
    for c in own:
        c.start()
    for i in range(1, parts):
        for n in range(2):
            kv_swap(i, n).start()
    for i in range(1, parts):
        q_swap(i).start()

    def lead(level, tile, n):
        win = wins[n][1]
        first, at, _ = leads[level]
        below = leads[level - 1][1] - leads[level - 1][0] if level else 0
        return remote(
            win.at[window_rows(below + tile)],
            win.at[window_rows(at + tile - first)],
            zs.at[level, n, tile],
            zr.at[level, n, tile],
            me + parts,
        )

    def lead_arrival(level, tile, n):
        first, at, _ = leads[level]
        win = wins[n][1].at[window_rows(at + tile - first)]
        return remote(win, win, zs.at[level, n, tile], zr.at[level, n, tile], me + parts)

    def send_lead(level, tile):
        @pl.when(has_next & (group >= level))
        def _():
            for n in range(2):
                lead(level, tile, n).start()

    order = list(range(parts - 1, -1, -1))
    for c in own[:2]:
        c.wait()
    for tile in order:
        @pl.when(place != tile)
        def _():
            for n in range(2):
                kv_arrival((place + parts - tile) % parts, n).wait_recv()

        send_lead(0, tile)
    for level in range(len(leads)):
        for tile in order:
            if tile < leads[level][0]:
                continue

            @pl.when(group > level)
            def _():
                for n in range(2):
                    lead_arrival(level, tile, n).wait_recv()

            if level + 1 < len(leads) and tile >= leads[level + 1][0]:
                send_lead(level + 1, tile)
    own[2].wait()
    for i in range(1, parts):
        q_arrival(i).wait_recv()
        q_swap(i).wait_send()
        for n in range(2):
            kv_swap(i, n).wait_send()
    for level in range(len(leads)):
        @pl.when(has_next & (group >= level))
        def _():
            for tile in order:
                if tile >= leads[level][0]:
                    for n in range(2):
                        lead(level, tile, n).wait_send()


def gather(query, key, value, parts, heads, groups, leads, tiles):
    rows = query.shape[0]
    qw = query.shape[1] // parts
    hbm = pl.BlockSpec(memory_space=pl.ANY)
    dma = pltpu.SemaphoreType.DMA
    win = jax.ShapeDtypeStruct((tiles * rows, HEAD_DIM), key.dtype)
    return pl.pallas_call(
        functools.partial(gather_kernel, heads, parts, groups, leads),
        out_shape=[jax.ShapeDtypeStruct((parts, rows, qw), query.dtype), win, win],
        in_specs=[pl.BlockSpec(memory_space=pltpu.VMEM)] * 3,
        out_specs=[hbm] * 3,
        scratch_shapes=[
            dma((3,)),
            dma((parts,)),
            dma((parts,)),
            dma((2, parts)),
            dma((2, parts)),
            dma((len(leads), 2, parts)),
            dma((len(leads), 2, parts)),
        ],
        compiler_params=pltpu.CompilerParams(collective_id=0, has_side_effects=True),
        name="gather",
    )(query, key, value)


def join_kernel(parts, qw, me_ref, *rest):
    pieces, out, sems = rest[:parts], rest[parts], rest[parts + 1]
    copies = []
    for i in range(parts):
        cols = pl.ds(pl.multiple_of((me_ref[0] ^ i) * qw, qw), qw)
        copies.append(pltpu.make_async_copy(pieces[i], out.at[:, cols], sems.at[i]))
    for c in copies:
        c.start()
    for c in copies:
        c.wait()


def join_heads(place, pieces):
    parts = len(pieces)
    rows, qw = pieces[0].shape
    hbm = pl.BlockSpec(memory_space=pl.ANY)
    return pl.pallas_call(
        functools.partial(join_kernel, parts, qw),
        out_shape=jax.ShapeDtypeStruct((rows, qw * parts), pieces[0].dtype),
        in_specs=[pl.BlockSpec(memory_space=pltpu.SMEM)] + [pl.BlockSpec(memory_space=pltpu.VMEM)] * parts,
        out_specs=hbm,
        scratch_shapes=[pltpu.SemaphoreType.DMA((parts,))],
        name="join_heads",
    )(place, *pieces)


def attend_kernel(n, groups, rows, sel, cnt, ent, kbase, qbase, *refs):
    queries, bounds = refs[:n], refs[n : 2 * n]
    k_ref, v_ref = refs[2 * n : 2 * n + 2]
    outs = refs[2 * n + 2 : 3 * n + 2]
    qt_ref, m_ref, l_ref, acc_ref = refs[3 * n + 2 :]
    scale = HEAD_DIM ** (-0.5) * LOG2E

    def tile(t, j, masked):
        row = pl.multiple_of((ent[t, j] // 2) * rows, rows)
        k = k_ref[pl.ds(row, rows), :]
        vt = v_ref[pl.ds(row, rows), :].T
        if masked:
            kpos = kbase[t, j] + lax.broadcasted_iota(jnp.int32, (rows, rows), 0)
            qpos = qbase[t] + lax.broadcasted_iota(jnp.int32, (rows, rows), 1)
            visible = (kpos <= qpos) & (kpos >= bounds[t][0])
        for g in range(groups):
            s = jnp.dot(k, qt_ref[g], preferred_element_type=jnp.float32)
            if masked:
                s = jnp.where(visible, s, NEG)
            m_old = m_ref[g : g + 1]
            m_new = jnp.maximum(m_old, jnp.max(s, axis=0, keepdims=True))
            p = jnp.exp2((s - m_new) * scale)
            alpha = jnp.exp2((m_old - m_new) * scale)
            m_ref[g : g + 1] = m_new
            l_ref[g : g + 1] = l_ref[g : g + 1] * alpha + jnp.sum(p, axis=0, keepdims=True)
            o = jnp.dot(vt, p.astype(jnp.bfloat16), preferred_element_type=jnp.float32)
            acc_ref[g] = acc_ref[g] * alpha + o

    for t in range(n):
        m_ref[...] = jnp.full_like(m_ref, NEG)
        l_ref[...] = jnp.zeros_like(l_ref)
        acc_ref[...] = jnp.zeros_like(acc_ref)
        for g in range(groups):
            qt_ref[g] = queries[t][0, :, g * HEAD_DIM : (g + 1) * HEAD_DIM].T

        def step(j, carry):
            @pl.when(ent[t, j] % 2 == 1)
            def _():
                tile(t, j, True)

            @pl.when(ent[t, j] % 2 == 0)
            def _():
                tile(t, j, False)

            return carry

        lax.fori_loop(0, cnt[t], step, 0)
        for g in range(groups):
            o = acc_ref[g] / l_ref[g : g + 1]
            outs[t][:, g * HEAD_DIM : (g + 1) * HEAD_DIM] = o.astype(outs[t].dtype).T


def attend(tables, q_all, row_starts, k_win, v_win):
    n = tables[0].shape[0]
    _, rows, qw = q_all.shape
    groups = qw // HEAD_DIM

    def picked(t):
        return lambda i, sel, *_: (sel[t], 0, 0)

    def fixed(t):
        return lambda i, *_: (t, 0, 0)

    def whole(i, *_):
        return (0, 0)

    return pl.pallas_call(
        functools.partial(attend_kernel, n, groups, rows),
        out_shape=[jax.ShapeDtypeStruct((rows, qw), q_all.dtype)] * n,
        grid_spec=pltpu.PrefetchScalarGridSpec(
            num_scalar_prefetch=5,
            grid=(1,),
            in_specs=[pl.BlockSpec((1, rows, qw), picked(t)) for t in range(n)]
            + [pl.BlockSpec((1, 1, rows), fixed(t)) for t in range(n)]
            + [pl.BlockSpec(k_win.shape, whole)] * 2,
            out_specs=[pl.BlockSpec((rows, qw), whole)] * n,
            scratch_shapes=[
                pltpu.VMEM((groups, HEAD_DIM, rows), q_all.dtype),
                pltpu.VMEM((groups, rows), jnp.float32),
                pltpu.VMEM((groups, rows), jnp.float32),
                pltpu.VMEM((groups, HEAD_DIM, rows), jnp.float32),
            ],
        ),
        compiler_params=pltpu.CompilerParams(vmem_limit_bytes=48 * 2**20),
        cost_estimate=pl.CostEstimate(
            flops=n * 10 * 4 * rows * rows * qw, bytes_accessed=8 * 2**20, transcendentals=n * 5 * rows * rows * groups
        ),
        name="attend",
    )(*tables, *([q_all] * n), *([row_starts] * n), k_win, v_win)


def tile_tables(group, parts, rows, leads, q_order, doc_lengths, block_mask):
    starts = running_sum(doc_lengths)
    order = jnp.arange(parts, dtype=jnp.int32)
    q_tile = group * parts + q_order
    k_tile = jnp.concatenate(
        [group * parts + order] + [(group - back) * parts + order[first:] for first, _, back in leads]
    )
    count = k_tile.shape[0]
    per = BLOCK // rows
    qb, kb = q_tile // per, k_tile // per
    offset = qb[:, None] - kb[None, :]
    allowed = jnp.concatenate([jnp.ones((block_mask.shape[0], 1), jnp.int32), block_mask], axis=1)[qb]
    hit = jnp.arange(allowed.shape[1], dtype=jnp.int32)
    allow = jnp.sum(jnp.where(offset[:, :, None] == hit, allowed[:, None, :], 0), axis=-1)
    row_starts = start_of(q_tile[:, None] * rows + jnp.arange(rows, dtype=jnp.int32), starts)
    k_first = k_tile * rows
    live = (
        (k_tile >= 0)[None, :]
        & (k_tile[None, :] <= q_tile[:, None])
        & (allow == 1)
        & ((k_first + rows - 1)[None, :] >= row_starts[:, :1])
    )
    masked = (k_tile[None, :] == q_tile[:, None]) | (k_first[None, :] < row_starts[:, -1:])
    live = live.astype(jnp.int32)
    spot = running_sum(live)
    pick = (spot[:, None, :] == jnp.arange(count, dtype=jnp.int32)[None, :, None]) & (live[:, None, :] == 1)
    code = jnp.arange(count, dtype=jnp.int32)[None, :] * 2 + masked.astype(jnp.int32)
    entries = jnp.sum(jnp.where(pick, code[:, None, :], 0), axis=-1)
    k_base = jnp.sum(jnp.where(pick, k_first[None, None, :], 0), axis=-1)
    return (jnp.sum(live, axis=1), entries, k_base, q_tile * rows), row_starts[:, None, :]


def body(query_states, key_states, value_states, doc_lengths, block_mask):
    heads, ctxs = lax.axis_size("head"), lax.axis_size("ctx")
    devices = heads * ctxs
    parts = key_states.shape[1] // HEAD_DIM
    rows = query_states.shape[0]
    me = lax.axis_index("ctx") * heads + lax.axis_index("head")
    group, place = me // parts, me % parts

    span, tiles, leads = (block_mask.shape[1] * BLOCK) // rows, parts, []
    while span > 0:
        count = min(parts, span)
        leads.append((parts - count, tiles, len(leads) + 1))
        span, tiles = span - count, tiles + count

    q_all, k_win, v_win = gather(
        query_states, key_states, value_states, parts, heads, devices // parts, leads, tiles
    )
    q_order = jnp.arange(parts - 1, -1, -1, dtype=jnp.int32) ^ place
    tables, row_starts = tile_tables(group, parts, rows, leads, q_order, doc_lengths, block_mask)
    tables = (q_order, *tables)

    def swap(array, i):
        flat = [d % heads * ctxs + d // heads for d in range(devices)]
        return lax.ppermute(array, ("head", "ctx"), [(flat[d], flat[d ^ i]) for d in range(devices)])

    back = [None] * parts
    for first in range(0, parts, 2):
        stage = slice(first, first + 2)
        outs = attend([table[stage] for table in tables], q_all, row_starts[stage], k_win, v_win)
        for i, out in zip((parts - 1 - first, parts - 2 - first), outs):
            back[i] = swap(out, i) if i else out
    return join_heads(place.reshape(1).astype(jnp.int32), back)


def solution(mesh):
    placed = (P(AXES, None), P(AXES, None), P(AXES, None), P(), P())
    return jax.shard_map(body, mesh=mesh, in_specs=placed, out_specs=P(AXES, None), check_vma=False)
```
